32 devices in a mesh: groups: 2 (over y), blk: 8 (over z, x), sector: 2 (over core).
Axes of the slice: x: 2, y: 2, z: 4, core: 2. Of those that a mesh axis runs over, the one named last changes fastest.
Arguments:
- wavefunction: bfloat16 [4096, 768], P(('groups', 'blk')), parts along dimension 0
- env_left: bfloat16 [16, 8, 2, 256, 256], P(('groups', 'blk'), None, 'sector'), parts along dimension 0
- pattern: int32 [16, 8, 2], P(('groups', 'blk'), None, 'sector'), parts along dimension 0, may hold values 0 or 1
- env_right: bfloat16 [16, 2, 768, 768], P(('groups', 'blk'), 'sector'), parts along dimension 0
- energy: float32 [16], P(('groups', 'blk')), parts along dimension 0, may hold values from 0.5 to 2
- block_rows: int32 [16], P(('groups', 'blk')), parts along dimension 0, may hold values from 64 to 256, as said below
Outputs:
- residual: float32 [4096, 768], P(('groups', 'blk', 'sector')), parts along dimension 0
- rayleigh: float32 [2], P('groups'), parts along dimension 0
The draws below stay inside these ranges and needn't reach their ends.
There are 2 independent parts, one for each index of `groups`. The reference program is written for one: setup_inputs(seed, part) draws one part's arguments, and reference() takes and returns one part's arrays. A program takes and returns all parts, laid end to end along the dimension named above; each array names one. Nothing has to cross between parts.
Inputs may be any that keep to these rules, and one draw needn't show every extreme that they name: `block_rows`: rows of a block at or past its entry are padding.
All inputs are finite; a program needn't handle non-finite values. No bound on the sum of `pattern` on one device may be relied on, other than what follows from the above.
Results may differ from the reference program's by a relative error of at most 0.0003.
Values may be sent and summed in bfloat16 or wider, within the bound.
A program may use at most 64 MiB of HBM per device.

```python
import math
import jax
import jax.numpy as jnp
from jax import lax

M = 256
C = 768
NB = 8
LOOP = 8


def draw_wavefunction(key, part):
    key = jax.random.fold_in(key, 11)
    key_values, key_factor, key_common = jax.random.split(key, 3)
    block_index = jnp.arange(NB * M) // M
    ramp = 0.6 + 1.2 * block_index.astype(jnp.float32) / max(NB - 1, 1)
    factor = jnp.exp(jax.random.uniform(key_factor, (NB,), jnp.float32, -0.7, 0.7))
    values = jax.random.normal(key_values, (NB * M, C), jnp.float32)
    common = jax.random.normal(key_common, (M, C), jnp.float32)
    weight_common = 0.5
    values = values + weight_common * jnp.tile(common, (NB, 1))
    scales = ramp * factor[block_index]
    return (values * scales[:, None]).astype(jnp.bfloat16)


def draw_env_left(key, part):
    key = jax.random.fold_in(key, 13)
    spread = (LOOP * M // 2) ** (-0.5)
    noise = jnp.clip(jax.random.normal(key, (NB, LOOP, 2, M, M), jnp.float32), -6.0, 6.0)
    diagonal = (jnp.arange(M)[:, None] == jnp.arange(M)[None, :]).astype(jnp.float32)
    return (spread * noise + 0.1 * diagonal).astype(jnp.bfloat16)


def draw_env_right(key, part):
    key = jax.random.fold_in(key, 14)
    spread = C ** (-0.5)
    noise = jnp.clip(jax.random.normal(key, (NB, 2, C, C), jnp.float32), -6.0, 6.0)
    diagonal = (jnp.arange(C)[:, None] == jnp.arange(C)[None, :]).astype(jnp.float32)
    return (spread * noise + 0.1 * diagonal).astype(jnp.bfloat16)


def draw_block_rows(key, part):
    key = jax.random.fold_in(key, 12)
    counts = jax.random.randint(key, (NB,), M // 4, M + 1, dtype=jnp.int32)
    return counts.at[0].set(M)


def plant(result, key, low, top_value):
    spot = [jax.random.randint(jax.random.fold_in(key, axis), (), 0, length) for axis, length in enumerate(result.shape)]
    longest = result.shape.index(max(result.shape))
    beside = spot[:longest] + [(spot[longest] + 1) % result.shape[longest]] + spot[longest + 1:]
    return result.at[tuple(spot)].set(low).at[tuple(beside)].set(top_value)


def block_scale(rng, extent, cuts, low, high):
    def one(dim, blocks):
        steps = jax.random.uniform(jax.random.fold_in(jax.random.fold_in(rng, 6), dim), (blocks,), jnp.float32, low / len(cuts), high / len(cuts))
        return jnp.repeat(jnp.exp(steps), extent[dim] // blocks).reshape((-1,) + (1,) * (len(extent) - dim - 1))

    factor_of = one(*cuts[0])
    for cut in cuts[1:]:
        factor_of = factor_of * one(*cut)
    return factor_of


def setup_inputs(seed: int = 0, part: int = 0) -> dict:
    key_list = jax.random.split(jax.random.key(seed), 7)
    part_splits = jax.random.split(jax.random.fold_in(key_list[6], part), 7)
    return {
        "wavefunction": draw_wavefunction(jax.random.fold_in(jax.random.fold_in(key_list[6], part), 71), part),
        "env_left": draw_env_left(jax.random.fold_in(jax.random.fold_in(key_list[6], part), 71), part),
        "pattern": plant((jax.random.randint(part_splits[2], (NB, LOOP, 2), 0, 2) < 1).astype(jnp.int32), jax.random.fold_in(part_splits[2], 1), 0, 1),
        "env_right": draw_env_right(jax.random.fold_in(jax.random.fold_in(key_list[6], part), 71), part),
        "energy": jnp.clip(jnp.exp(math.log(2.0) - 1.3862944 * jax.random.uniform(part_splits[4], (NB,), jnp.float32) ** block_scale(part_splits[4], (NB,), ((0, 8),), -0.2, 0.2)), 0.5, 2.0),
        "block_rows": draw_block_rows(jax.random.fold_in(jax.random.fold_in(key_list[6], part), 71), part),
    }


def reference(wavefunction, env_left, pattern, env_right, energy, block_rows):
    live_rows = (jnp.arange(M)[None, :] < block_rows[:, None]).astype(jnp.bfloat16)
    blocks = wavefunction.reshape(NB, M, C) * live_rows[:, :, None]
    offsets = jnp.arange(LOOP, dtype=jnp.int32) - LOOP // 2

    def owner_sigma(index):
        sources = ((index + offsets) % NB).astype(jnp.int32)
        window_blocks = jnp.take(blocks, sources, axis=0).astype(jnp.float32)
        coupled = (env_left[index] * pattern[index][:, :, None, None].astype(jnp.bfloat16)).astype(jnp.float32)
        reduced = jnp.einsum("jcab,jbd->cad", coupled, window_blocks, precision=lax.Precision.HIGHEST)
        products = jnp.einsum("cad,cde->cae", reduced, env_right[index].astype(jnp.float32), precision=lax.Precision.HIGHEST)
        own_block = lax.dynamic_index_in_dim(blocks, index, 0, keepdims=False).astype(jnp.float32)
        sigma_one = jnp.sum(products, axis=0) + energy[index] * own_block
        return sigma_one * live_rows[index][:, None].astype(jnp.float32)

    sigma_all = lax.map(owner_sigma, jnp.arange(NB, dtype=jnp.int32))
    blocks_wide = blocks.astype(jnp.float32)
    rayleigh = jnp.sum(blocks_wide * sigma_all) / jnp.sum(blocks_wide * blocks_wide)
    residual = (sigma_all - rayleigh * blocks_wide).reshape(NB * M, C)
    return residual, rayleigh.reshape(1)
```

```python
import functools

import jax
import jax.numpy as jnp
from jax import lax
from jax.experimental import pallas as pl
from jax.experimental.pallas import tpu as pltpu
from jax.sharding import PartitionSpec as P

DOWN, UP, ACROSS = 0, 1, 2


def from_behind(value, axis, steps):
    count = lax.axis_size(axis)
    pairs = [(source, (source + steps) % count) for source in range(count)]
    return lax.ppermute(value, axis, pairs)


def ring_shards(wavefunction, env_left, pattern, env_right, energy, block_rows):
    rows_pad = env_left.shape[-1]
    loop_len = env_left.shape[1]
    middle = loop_len // 2
    half_rows = rows_pad // 2
    live_rows = (jnp.arange(rows_pad) < block_rows[0]).astype(jnp.bfloat16)
    own_block = wavefunction * live_rows[:, None]
    coupled = env_left[0, :, 0] * pattern[0, :, 0].astype(jnp.bfloat16)[:, None, None]
    core_index = lax.axis_index("sector")
    own_half = lax.dynamic_slice_in_dim(own_block, core_index * half_rows, half_rows, 0)

    def add_term(summed_now, slot, pieces):
        term_env = lax.dynamic_index_in_dim(coupled, slot, 0, keepdims=False)
        return summed_now + jnp.dot(term_env, pieces, preferred_element_type=jnp.float32)

    moving = from_behind(own_block, "blk", middle)
    summed = jnp.zeros((rows_pad, own_block.shape[1]), jnp.float32)
    summed = add_term(summed, 0, moving)

    def advance(turn, state):
        moving_now, summed_now = state
        moving_now = from_behind(moving_now, "blk", -1)
        return (moving_now, add_term(summed_now, turn, moving_now))

    moving, summed = lax.fori_loop(1, loop_len, advance, (moving, summed))
    partial_sigma = jnp.dot(
        summed,
        env_right[0, 0].astype(jnp.float32),
        precision=lax.Precision.HIGHEST,
        preferred_element_type=jnp.float32,
    )
    summed_terms = lax.psum(partial_sigma, "sector")
    mine = lax.dynamic_slice_in_dim(summed_terms, core_index * half_rows, half_rows, 0)
    live_half = lax.dynamic_slice_in_dim(live_rows, core_index * half_rows, half_rows, 0).astype(
        jnp.float32
    )
    own_wide = own_half.astype(jnp.float32)
    sigma_half = (mine + energy[0] * own_wide) * live_half[:, None]
    correlation, norm_sq = lax.psum(
        (jnp.sum(own_wide * sigma_half), jnp.sum(own_wide * own_wide)), ("blk", "sector")
    )
    rayleigh = correlation / norm_sq
    residual = sigma_half - rayleigh * own_wide
    return (residual, rayleigh.reshape(1))


def row_pieces(rows):
    across = rows * 3 // 16 // 16 * 16
    line = rows - across
    front = (line // 2 + 15) // 16 * 16
    return [(0, front), (front, line - front)], [(line, across)]


def kernel(
    n,
    wave_hbm,
    left_hbm,
    right_hbm,
    pattern,
    energy,
    block_rows,
    residual,
    rayleigh,
    wave,
    blocks,
    left,
    right,
    acc,
    part_out,
    part_in,
    part_own,
    stats,
    local_sem,
    send_sem,
    recv_sem,
    pair_send,
    pair_recv,
    stat_send,
    stat_recv,
):
    lines = n // 2
    rows, cols = wave.shape
    half_rows, half_cols = rows // 2, cols // 2
    middle = n // 2
    core = lax.axis_index("sector")
    me = lax.axis_index("blk")
    other = 1 - core
    z, x = me // 2, me % 2
    beside = me + 1 - 2 * x
    rank = me * 2 + core
    line_first, across_first = row_pieces(rows)
    pieces = line_first + across_first
    n_line = len(line_first)
    has = {DOWN: z > 0, UP: z < lines - 1, ACROSS: None}
    toward = {DOWN: me - 2, UP: me + 2, ACROSS: beside}

    wave_copy = pltpu.make_async_copy(wave_hbm, wave, local_sem.at[0])
    left_copy = pltpu.make_async_copy(
        left_hbm.at[0, :, 0], left.at[:, pl.ds(core * rows, rows)], local_sem.at[1]
    )
    right_copy = pltpu.make_async_copy(
        right_hbm.at[0, 0, pl.ds(core * half_cols, half_cols)], right.at[core], local_sem.at[2]
    )
    wave_copy.start()
    left_copy.start()
    right_copy.start()

    barrier = pltpu.get_barrier_semaphore()
    for step in range(1, 2 * n):
        peer = lax.rem(rank + step, 2 * n)
        pl.semaphore_signal(
            barrier,
            inc=1,
            device_id={"blk": peer // 2, "sector": peer % 2},
            device_id_type=pl.DeviceIdType.MESH,
        )

    wave_copy.wait()
    row_ids = lax.broadcasted_iota(jnp.int32, (rows, cols), 0)
    wave[...] = jnp.where(row_ids < block_rows[0], wave[...].astype(jnp.float32), 0.0).astype(
        wave.dtype
    )
    blocks[me] = wave[:, pl.ds(pl.multiple_of(core * half_cols, half_cols), half_cols)]
    pl.semaphore_wait(barrier, 2 * n - 1)

    sent = []

    def under(condition, action):
        if condition is None:
            action()
        else:
            pl.when(condition)(action)

    def both(first, second):
        if first is None:
            return second
        if second is None:
            return first
        return jnp.logical_and(first, second)

    def block_copy(block, piece, way):
        start, size = pieces[piece]
        part = blocks.at[block, pl.ds(start, size)]
        return pltpu.make_async_remote_copy(
            src_ref=part,
            dst_ref=part,
            send_sem=send_sem.at[block, piece, way],
            recv_sem=recv_sem.at[block, piece],
            device_id={"blk": toward[way], "sector": core},
            device_id_type=pl.DeviceIdType.MESH,
        )

    def send(block, piece, way, condition=None):
        condition = both(condition, has[way])
        under(condition, lambda: block_copy(block, piece, way).start())
        sent.append((block, piece, way, condition))

    def receive(block, piece, condition=None):
        under(condition, lambda: block_copy(block, piece, ACROSS).wait_recv())

    for piece in range(n_line):
        for way in (DOWN, UP, ACROSS):
            send(me, piece, way)
    for piece in range(n_line, len(pieces)):
        for way in (ACROSS, DOWN, UP):
            send(me, piece, way)

    def pair_copy(source, target, index):
        return pltpu.make_async_remote_copy(
            src_ref=source,
            dst_ref=target,
            send_sem=pair_send.at[index],
            recv_sem=pair_recv.at[index],
            device_id={"sector": other},
            device_id_type=pl.DeviceIdType.MESH,
        )

    left_copy.wait()
    for slot in range(n):
        mine = left[slot, pl.ds(core * rows, rows)].astype(jnp.float32)
        left[slot, pl.ds(core * rows, rows)] = (
            mine * pattern[0, slot, 0].astype(jnp.float32)
        ).astype(left.dtype)
    own_left = left.at[:, pl.ds(core * rows, rows)]
    left_out = pair_copy(own_left, own_left, 0)
    left_out.start()
    right_out = pair_copy(
        right_hbm.at[0, 0, pl.ds(other * half_cols, half_cols)], right.at[core], 1
    )
    right_out.start()

    def accumulate(block, condition=None, fresh=False):
        def action():
            slot = lax.rem(block - me + middle + n, n)
            product = jnp.dot(left[slot], blocks[block], preferred_element_type=jnp.float32)
            acc[...] = product if fresh else acc[...] + product

        under(condition, action)

    def forward(distance):
        sides = (
            (me + 2 * distance, z + distance < lines, DOWN),
            (me - 2 * distance, z >= distance, UP),
        )
        for piece in range(n_line):
            for block, condition, way in sides:
                receive(block, piece, condition)
                send(block, piece, way, condition)
                send(block, piece, ACROSS, condition)
        for piece in range(n_line, len(pieces)):
            if distance == 1:
                receive(beside, piece)
                send(beside, piece, DOWN)
                send(beside, piece, UP)
            for block, condition, way in sides:
                for source in (block, block + 1 - 2 * x):
                    receive(source, piece, condition)
                    send(source, piece, way, condition)

    def compute(distance):
        if distance < lines:
            accumulate(me + 2 * distance, z + distance < lines)
            accumulate(me - 2 * distance, z >= distance)
        near = distance - 1
        sides = [(beside, None)]
        if near:
            sides = [(beside + 2 * near, z + near < lines), (beside - 2 * near, z >= near)]
        for block, condition in sides:
            for piece in range(n_line):
                receive(block, piece, condition)
            accumulate(block, condition)

    forward(1)
    left_out.wait_recv()
    accumulate(me, fresh=True)
    for distance in range(2, lines):
        forward(distance)
        compute(distance - 1)
    compute(lines - 1)
    compute(lines)

    right_copy.wait()
    right_out.wait_recv()

    def finish(first):
        total = None
        for term in range(2):
            wide = acc[pl.ds(pl.multiple_of(term * rows + first, half_rows), half_rows)]
            high = wide.astype(jnp.bfloat16)
            low = (wide - high.astype(jnp.float32)).astype(jnp.bfloat16)
            both_parts = jnp.concatenate([high, low], axis=0)
            product = jnp.dot(both_parts, right[term], preferred_element_type=jnp.float32)
            product = product[:half_rows] + product[half_rows:]
            total = product if total is None else total + product
        return total

    def lanes(values):
        summed = values[:, 0:128]
        for column in range(128, cols, 128):
            summed = summed + values[:, column : column + 128]
        return jnp.sum(summed, axis=0, keepdims=True)

    first_other = pl.multiple_of(other * half_rows, half_rows)
    first_own = pl.multiple_of(core * half_rows, half_rows)
    partial_other = finish(first_other)
    part_out[...] = partial_other
    part_copy = pair_copy(part_out, part_in, 2)
    part_copy.start()
    partial_own = finish(first_own)
    part_own[...] = partial_own
    wave_other = wave[pl.ds(first_other, half_rows)].astype(jnp.float32)
    wave_own = wave[pl.ds(first_own, half_rows)].astype(jnp.float32)
    norm = lanes(wave_own * wave_own)
    correlation = lanes(part_out[...] * wave_other + part_own[...] * wave_own) + energy[0] * norm
    stat_rows = lax.broadcasted_iota(jnp.int32, (8, 128), 0)
    stats[rank] = jnp.where(stat_rows == 0, correlation, jnp.where(stat_rows == 1, norm, 0.0))

    def stat_copy(peer, slot):
        return pltpu.make_async_remote_copy(
            src_ref=stats.at[slot],
            dst_ref=stats.at[slot],
            send_sem=stat_send.at[peer],
            recv_sem=stat_recv.at[slot],
            device_id={"blk": peer // 2, "sector": peer % 2},
            device_id_type=pl.DeviceIdType.MESH,
        )

    for step in range(1, 2 * n):
        stat_copy(lax.rem(rank + step, 2 * n), rank).start()

    part_copy.wait_recv()
    live = lax.broadcasted_iota(jnp.int32, (half_rows, cols), 0) + first_own < block_rows[0]
    part_own[...] = jnp.where(
        live, part_own[...] + part_in[...] + energy[0] * wave_own, 0.0
    )
    for step in range(1, 2 * n):
        peer = lax.rem(rank + step, 2 * n)
        stat_copy(peer, peer).wait_recv()
    total = jnp.sum(stats[...], axis=0)
    totals = jnp.sum(total, axis=1, keepdims=True)
    quotient = totals[0:1] / totals[1:2]
    rayleigh[0] = quotient[0, 0]
    residual[...] = part_own[...] - quotient * wave_own

    for block, piece, way, condition in sent:
        under(condition, lambda: block_copy(block, piece, way).wait_send())
    left_out.wait_send()
    right_out.wait_send()
    part_copy.wait_send()
    for step in range(1, 2 * n):
        stat_copy(lax.rem(rank + step, 2 * n), rank).wait_send()


def line_shards(wavefunction, env_left, pattern, env_right, energy, block_rows):
    n = lax.axis_size("blk")
    rows, cols = wavefunction.shape
    half_rows, half_cols = rows // 2, cols // 2
    line_first, across_first = row_pieces(rows)
    count = len(line_first) + len(across_first)
    bf16, f32 = jnp.bfloat16, jnp.float32
    dma = pltpu.SemaphoreType.DMA
    smem = pl.BlockSpec(memory_space=pltpu.SMEM)
    hbm = pl.BlockSpec(memory_space=pl.ANY)
    residual, rayleigh = pl.pallas_call(
        functools.partial(kernel, n),
        out_shape=(
            jax.ShapeDtypeStruct((half_rows, cols), f32),
            jax.ShapeDtypeStruct((1,), f32),
        ),
        in_specs=[hbm, hbm, hbm, smem, smem, smem],
        out_specs=(pl.BlockSpec(memory_space=pltpu.VMEM), smem),
        scratch_shapes=[
            pltpu.VMEM((rows, cols), bf16),
            pltpu.VMEM((n, rows, half_cols), bf16),
            pltpu.VMEM((n, 2 * rows, rows), bf16),
            pltpu.VMEM((2, half_cols, cols), bf16),
            pltpu.VMEM((2 * rows, half_cols), f32),
            pltpu.VMEM((half_rows, cols), f32),
            pltpu.VMEM((half_rows, cols), f32),
            pltpu.VMEM((half_rows, cols), f32),
            pltpu.VMEM((2 * n, 8, 128), f32),
            dma((3,)),
            dma((n, count, 3)),
            dma((n, count)),
            dma((3,)),
            dma((3,)),
            dma((2 * n,)),
            dma((2 * n,)),
        ],
        compiler_params=pltpu.CompilerParams(
            collective_id=0, has_side_effects=True, vmem_limit_bytes=40 * 1024 * 1024
        ),
        cost_estimate=pl.CostEstimate(
            flops=6 * rows * rows * cols * n, bytes_accessed=4 * n * rows * rows, transcendentals=0
        ),
    )(wavefunction, env_left, env_right, pattern, energy, block_rows)
    return residual, rayleigh


def solution(mesh):
    blk = mesh.shape["blk"]

    def shards(wavefunction, env_left, pattern, env_right, energy, block_rows):
        all_coupled = env_left.shape[1] == blk and blk % 2 == 0
        body = line_shards if all_coupled else ring_shards
        return body(wavefunction, env_left, pattern, env_right, energy, block_rows)

    return jax.shard_map(
        shards,
        mesh=mesh,
        in_specs=(
            P(("groups", "blk"), None),
            P(("groups", "blk"), None, "sector", None, None),
            P(("groups", "blk"), None, "sector"),
            P(("groups", "blk"), "sector", None, None),
            P(("groups", "blk")),
            P(("groups", "blk")),
        ),
        out_specs=(P(("groups", "blk", "sector"), None), P("groups")),
        check_vma=False,
    )
```

```python
import functools

import jax
import jax.numpy as jnp
from jax import lax
from jax.experimental import pallas as pl
from jax.experimental.pallas import tpu as pltpu
from jax.sharding import PartitionSpec as P

DOWN, UP, ACROSS = 0, 1, 2


def from_behind(value, axis, steps):
    count = lax.axis_size(axis)
    pairs = [(source, (source + steps) % count) for source in range(count)]
    return lax.ppermute(value, axis, pairs)


def ring_shards(wavefunction, env_left, pattern, env_right, energy, block_rows):
    rows_pad = env_left.shape[-1]
    loop_len = env_left.shape[1]
    middle = loop_len // 2
    half_rows = rows_pad // 2
    live_rows = (jnp.arange(rows_pad) < block_rows[0]).astype(jnp.bfloat16)
    own_block = wavefunction * live_rows[:, None]
    coupled = env_left[0, :, 0] * pattern[0, :, 0].astype(jnp.bfloat16)[:, None, None]
    core_index = lax.axis_index("sector")
    own_half = lax.dynamic_slice_in_dim(own_block, core_index * half_rows, half_rows, 0)

    def add_term(summed_now, slot, pieces):
        term_env = lax.dynamic_index_in_dim(coupled, slot, 0, keepdims=False)
        return summed_now + jnp.dot(term_env, pieces, preferred_element_type=jnp.float32)

    moving = from_behind(own_block, "blk", middle)
    summed = jnp.zeros((rows_pad, own_block.shape[1]), jnp.float32)
    summed = add_term(summed, 0, moving)

    def advance(turn, state):
        moving_now, summed_now = state
        moving_now = from_behind(moving_now, "blk", -1)
        return (moving_now, add_term(summed_now, turn, moving_now))

    moving, summed = lax.fori_loop(1, loop_len, advance, (moving, summed))
    partial_sigma = jnp.dot(
        summed,
        env_right[0, 0].astype(jnp.float32),
        precision=lax.Precision.HIGHEST,
        preferred_element_type=jnp.float32,
    )
    summed_terms = lax.psum(partial_sigma, "sector")
    mine = lax.dynamic_slice_in_dim(summed_terms, core_index * half_rows, half_rows, 0)
    live_half = lax.dynamic_slice_in_dim(live_rows, core_index * half_rows, half_rows, 0).astype(
        jnp.float32
    )
    own_wide = own_half.astype(jnp.float32)
    sigma_half = (mine + energy[0] * own_wide) * live_half[:, None]
    correlation, norm_sq = lax.psum(
        (jnp.sum(own_wide * sigma_half), jnp.sum(own_wide * own_wide)), ("blk", "sector")
    )
    rayleigh = correlation / norm_sq
    residual = sigma_half - rayleigh * own_wide
    return (residual, rayleigh.reshape(1))


def kernel(
    n,
    wave_hbm,
    left_hbm,
    right_hbm,
    pattern,
    energy,
    block_rows,
    residual,
    rayleigh,
    wave,
    blocks,
    left,
    right,
    acc,
    part_out,
    part_in,
    part_own,
    stats,
    local_sem,
    send_sem,
    recv_sem,
    pair_send,
    pair_recv,
    stat_send,
    stat_recv,
):
    lines = n // 2
    rows, cols = wave.shape
    half_rows, half_cols = rows // 2, cols // 2
    middle = n // 2
    core = lax.axis_index("sector")
    me = lax.axis_index("blk")
    other = 1 - core
    z, x = me // 2, me % 2
    beside = me + 1 - 2 * x
    rank = me * 2 + core
    at_end = jnp.logical_or(z == 0, z == lines - 1)
    has = {DOWN: z > 0, UP: z < lines - 1, ACROSS: None}
    toward = {DOWN: me - 2, UP: me + 2, ACROSS: beside}

    wave_copy = pltpu.make_async_copy(wave_hbm, wave, local_sem.at[0])
    left_copy = pltpu.make_async_copy(
        left_hbm.at[0, :, 0], left.at[:, pl.ds(core * rows, rows)], local_sem.at[1]
    )
    right_copy = pltpu.make_async_copy(
        right_hbm.at[0, 0, pl.ds(core * half_cols, half_cols)], right.at[core], local_sem.at[2]
    )
    wave_copy.start()
    left_copy.start()
    right_copy.start()

    barrier = pltpu.get_barrier_semaphore()
    def greet(block, which):
        pl.semaphore_signal(
            barrier,
            inc=1,
            device_id={"blk": block, "sector": which},
            device_id_type=pl.DeviceIdType.MESH,
        )

    greet(me, other)
    greet(beside, core)
    for way in (DOWN, UP):
        pl.when(has[way])(lambda: greet(toward[way], core))

    wave_copy.wait()
    row_ids = lax.broadcasted_iota(jnp.int32, (rows, cols), 0)
    wave[...] = jnp.where(row_ids < block_rows[0], wave[...].astype(jnp.float32), 0.0).astype(
        wave.dtype
    )
    blocks[me] = wave[:, pl.ds(pl.multiple_of(core * half_cols, half_cols), half_cols)]
    pl.semaphore_wait(barrier, 2 + has[DOWN].astype(jnp.int32) + has[UP].astype(jnp.int32))

    sent = []

    def under(condition, action):
        if condition is None:
            action()
        else:
            pl.when(condition)(action)

    def both(first, second):
        if first is None:
            return second
        if second is None:
            return first
        return jnp.logical_and(first, second)

    def block_copy(block, piece, way):
        part = blocks.at[block, pl.ds(piece * half_rows, half_rows)]
        return pltpu.make_async_remote_copy(
            src_ref=part,
            dst_ref=part,
            send_sem=send_sem.at[block, piece, way],
            recv_sem=recv_sem.at[block, piece],
            device_id={"blk": toward[way], "sector": core},
            device_id_type=pl.DeviceIdType.MESH,
        )

    def send(block, piece, way, condition=None):
        condition = both(condition, has[way])
        under(condition, lambda: block_copy(block, piece, way).start())
        sent.append((block, piece, way, condition))

    def receive(block, piece, condition=None):
        under(condition, lambda: block_copy(block, piece, ACROSS).wait_recv())

    for piece in range(2):
        send(me, piece, DOWN)
        send(me, piece, UP)
        send(me, 1 - piece, ACROSS)

    def pair_copy(source, target, index):
        return pltpu.make_async_remote_copy(
            src_ref=source,
            dst_ref=target,
            send_sem=pair_send.at[index],
            recv_sem=pair_recv.at[index],
            device_id={"sector": other},
            device_id_type=pl.DeviceIdType.MESH,
        )

    left_copy.wait()
    for slot in range(n):
        mine = left[slot, pl.ds(core * rows, rows)].astype(jnp.float32)
        left[slot, pl.ds(core * rows, rows)] = (
            mine * pattern[slot].astype(jnp.float32)
        ).astype(left.dtype)
    own_left = left.at[:, pl.ds(core * rows, rows)]
    left_out = pair_copy(own_left, own_left, 0)
    left_out.start()
    right_out = pair_copy(
        right_hbm.at[0, 0, pl.ds(other * half_cols, half_cols)], right.at[core], 1
    )
    right_out.start()

    def accumulate(block, condition=None, fresh=False):
        def action():
            slot = lax.rem(block - me + middle + n, n)
            product = jnp.dot(left[slot], blocks[block], preferred_element_type=jnp.float32)
            acc[...] = product if fresh else acc[...] + product

        under(condition, action)

    def ends(distance):
        return (
            (beside + 2 * distance, z + distance == lines - 1, DOWN),
            (beside - 2 * distance, z == distance, UP),
        )

    def sides(block, distance):
        if distance == 0:
            return ((block, None, None),)
        return (
            (block + 2 * distance, z + distance < lines, DOWN),
            (block - 2 * distance, z >= distance, UP),
        )

    def forward(distance):
        for piece in range(2):
            for block, condition, way in sides(me, distance):
                receive(block, piece, condition)
                send(block, piece, way, condition)
                if piece == 0:
                    send(block, piece, ACROSS, condition)
            if piece == 1:
                for block, condition, way in sides(me, distance):
                    inner = both(condition, is_inner(distance, way))
                    send(block, piece, ACROSS, inner)
            if distance == 1 and piece == 0:
                receive(beside, 1)
                send(beside, 1, DOWN, at_end)
                send(beside, 1, UP, at_end)

    def is_inner(distance, way):
        return z + distance < lines - 1 if way == DOWN else z > distance

    def forward_ends(distance):
        for block, condition, way in ends(distance):
            receive(block, 1, condition)
            send(block, 1, way, condition)

    def own_line(distance):
        for block, condition, _ in sides(me, distance):
            accumulate(block, condition)

    def other_line(distance):
        for block, condition, way in sides(beside, distance):
            receive(block, 0, condition)
            if distance:
                receive(block, 1, both(condition, is_inner(distance, way)))
            accumulate(block, condition)

    for distance in range(1, lines):
        forward(distance)
        if distance < lines - 1:
            forward_ends(distance)
        if distance == 1:
            left_out.wait_recv()
            accumulate(me, fresh=True)
        else:
            other_line(distance - 2)
        own_line(distance)
    if lines > 1:
        other_line(lines - 2)
        forward_ends(lines - 1)
    else:
        left_out.wait_recv()
        accumulate(me, fresh=True)
        receive(beside, 1)
    other_line(lines - 1)

    right_copy.wait()
    right_out.wait_recv()

    def finish(first):
        total = None
        for term in range(2):
            wide = acc[pl.ds(pl.multiple_of(term * rows + first, half_rows), half_rows)]
            high = wide.astype(jnp.bfloat16)
            low = (wide - high.astype(jnp.float32)).astype(jnp.bfloat16)
            both_parts = jnp.concatenate([high, low], axis=0)
            product = jnp.dot(both_parts, right[term], preferred_element_type=jnp.float32)
            product = product[:half_rows] + product[half_rows:]
            total = product if total is None else total + product
        return total

    def lanes(values):
        summed = values[:, 0:128]
        for column in range(128, cols, 128):
            summed = summed + values[:, column : column + 128]
        return jnp.sum(summed, axis=0, keepdims=True)

    first_other = pl.multiple_of(other * half_rows, half_rows)
    first_own = pl.multiple_of(core * half_rows, half_rows)
    partial_other = finish(first_other)
    part_out[...] = partial_other
    part_copy = pair_copy(part_out, part_in, 2)
    part_copy.start()
    partial_own = finish(first_own)
    part_own[...] = partial_own
    wave_other = wave[pl.ds(first_other, half_rows)].astype(jnp.float32)
    wave_own = wave[pl.ds(first_own, half_rows)].astype(jnp.float32)
    norm = lanes(wave_own * wave_own)
    correlation = lanes(part_out[...] * wave_other + part_own[...] * wave_own) + energy[0] * norm
    stat_rows = lax.broadcasted_iota(jnp.int32, (8, 128), 0)
    stats[rank] = jnp.where(stat_rows == 0, correlation, jnp.where(stat_rows == 1, norm, 0.0))

    def stat_copy(peer, slot):
        return pltpu.make_async_remote_copy(
            src_ref=stats.at[slot],
            dst_ref=stats.at[slot],
            send_sem=stat_send.at[peer],
            recv_sem=stat_recv.at[slot],
            device_id={"blk": peer // 2, "sector": peer % 2},
            device_id_type=pl.DeviceIdType.MESH,
        )

    for step in range(1, 2 * n):
        stat_copy(lax.rem(rank + step, 2 * n), rank).start()

    part_copy.wait_recv()
    live = lax.broadcasted_iota(jnp.int32, (half_rows, cols), 0) + first_own < block_rows[0]
    part_own[...] = jnp.where(
        live, part_own[...] + part_in[...] + energy[0] * wave_own, 0.0
    )
    for step in range(1, 2 * n):
        peer = lax.rem(rank + step, 2 * n)
        stat_copy(peer, peer).wait_recv()
    total = jnp.sum(stats[...], axis=0)
    totals = jnp.sum(total, axis=1, keepdims=True)
    quotient = totals[0:1] / totals[1:2]
    rayleigh[0] = quotient[0, 0]
    residual[...] = part_own[...] - quotient * wave_own

    for block, piece, way, condition in sent:
        under(condition, lambda: block_copy(block, piece, way).wait_send())
    left_out.wait_send()
    right_out.wait_send()
    part_copy.wait_send()
    for step in range(1, 2 * n):
        stat_copy(lax.rem(rank + step, 2 * n), rank).wait_send()


def line_shards(wavefunction, env_left, pattern, env_right, energy, block_rows):
    n = lax.axis_size("blk")
    rows, cols = wavefunction.shape
    half_rows, half_cols = rows // 2, cols // 2
    bf16, f32 = jnp.bfloat16, jnp.float32
    dma = pltpu.SemaphoreType.DMA
    smem = pl.BlockSpec(memory_space=pltpu.SMEM)
    hbm = pl.BlockSpec(memory_space=pltpu.HBM)
    residual, rayleigh = pl.pallas_call(
        functools.partial(kernel, n),
        out_shape=(
            jax.ShapeDtypeStruct((half_rows, cols), f32),
            jax.ShapeDtypeStruct((1,), f32),
        ),
        in_specs=[hbm, hbm, hbm, smem, smem, smem],
        out_specs=(pl.BlockSpec(memory_space=pltpu.VMEM), smem),
        scratch_shapes=[
            pltpu.VMEM((rows, cols), bf16),
            pltpu.VMEM((n, rows, half_cols), bf16),
            pltpu.VMEM((n, 2 * rows, rows), bf16),
            pltpu.VMEM((2, half_cols, cols), bf16),
            pltpu.VMEM((2 * rows, half_cols), f32),
            pltpu.VMEM((half_rows, cols), f32),
            pltpu.VMEM((half_rows, cols), f32),
            pltpu.VMEM((half_rows, cols), f32),
            pltpu.VMEM((2 * n, 8, 128), f32),
            dma((3,)),
            dma((n, 2, 3)),
            dma((n, 2)),
            dma((3,)),
            dma((3,)),
            dma((2 * n,)),
            dma((2 * n,)),
        ],
        compiler_params=pltpu.CompilerParams(
            collective_id=0, has_side_effects=True, vmem_limit_bytes=60 * 1024 * 1024
        ),
        cost_estimate=pl.CostEstimate(
            flops=6 * rows * rows * cols * n, bytes_accessed=4 * n * rows * rows, transcendentals=0
        ),
    )(wavefunction, env_left, env_right, pattern.reshape(n), energy, block_rows)
    return residual, rayleigh


def solution(mesh):
    blk = mesh.shape["blk"]

    def shards(wavefunction, env_left, pattern, env_right, energy, block_rows):
        all_coupled = env_left.shape[1] == blk and blk % 2 == 0
        body = line_shards if all_coupled else ring_shards
        return body(wavefunction, env_left, pattern, env_right, energy, block_rows)

    return jax.shard_map(
        shards,
        mesh=mesh,
        in_specs=(
            P(("groups", "blk"), None),
            P(("groups", "blk"), None, "sector", None, None),
            P(("groups", "blk"), None, "sector"),
            P(("groups", "blk"), "sector", None, None),
            P(("groups", "blk")),
            P(("groups", "blk")),
        ),
        out_specs=(P(("groups", "blk", "sector"), None), P("groups")),
        check_vma=False,
    )
```

```python
import functools

import jax
import jax.numpy as jnp
from jax import lax
from jax.experimental import pallas as pl
from jax.experimental.pallas import tpu as pltpu
from jax.sharding import PartitionSpec as P

DOWN, UP, ACROSS = 0, 1, 2


def from_behind(value, axis, steps):
    count = lax.axis_size(axis)
    pairs = [(source, (source + steps) % count) for source in range(count)]
    return lax.ppermute(value, axis, pairs)


def ring_shards(wavefunction, env_left, pattern, env_right, energy, block_rows):
    rows_pad = env_left.shape[-1]
    loop_len = env_left.shape[1]
    middle = loop_len // 2
    half_rows = rows_pad // 2
    live_rows = (jnp.arange(rows_pad) < block_rows[0]).astype(jnp.bfloat16)
    own_block = wavefunction * live_rows[:, None]
    coupled = env_left[0, :, 0] * pattern[0, :, 0].astype(jnp.bfloat16)[:, None, None]
    core_index = lax.axis_index("sector")
    own_half = lax.dynamic_slice_in_dim(own_block, core_index * half_rows, half_rows, 0)

    def add_term(summed_now, slot, pieces):
        term_env = lax.dynamic_index_in_dim(coupled, slot, 0, keepdims=False)
        return summed_now + jnp.dot(term_env, pieces, preferred_element_type=jnp.float32)

    moving = from_behind(own_block, "blk", middle)
    summed = jnp.zeros((rows_pad, own_block.shape[1]), jnp.float32)
    summed = add_term(summed, 0, moving)

    def advance(turn, state):
        moving_now, summed_now = state
        moving_now = from_behind(moving_now, "blk", -1)
        return (moving_now, add_term(summed_now, turn, moving_now))

    moving, summed = lax.fori_loop(1, loop_len, advance, (moving, summed))
    partial_sigma = jnp.dot(
        summed,
        env_right[0, 0].astype(jnp.float32),
        precision=lax.Precision.HIGHEST,
        preferred_element_type=jnp.float32,
    )
    summed_terms = lax.psum(partial_sigma, "sector")
    mine = lax.dynamic_slice_in_dim(summed_terms, core_index * half_rows, half_rows, 0)
    live_half = lax.dynamic_slice_in_dim(live_rows, core_index * half_rows, half_rows, 0).astype(
        jnp.float32
    )
    own_wide = own_half.astype(jnp.float32)
    sigma_half = (mine + energy[0] * own_wide) * live_half[:, None]
    correlation, norm_sq = lax.psum(
        (jnp.sum(own_wide * sigma_half), jnp.sum(own_wide * own_wide)), ("blk", "sector")
    )
    rayleigh = correlation / norm_sq
    residual = sigma_half - rayleigh * own_wide
    return (residual, rayleigh.reshape(1))


def kernel(
    n,
    wave_hbm,
    left_hbm,
    right_hbm,
    pattern_hbm,
    energy_hbm,
    block_rows_hbm,
    residual,
    rayleigh,
    pattern,
    energy,
    block_rows,
    wave,
    blocks,
    left,
    right,
    acc,
    partial,
    part_in,
    stats,
    local_sem,
    send_sem,
    recv_sem,
    pair_send,
    pair_recv,
    stat_send,
    stat_recv,
):
    lines = n // 2
    rows, cols = wave.shape
    half_rows, half_cols = rows // 2, cols // 2
    middle = n // 2
    core = lax.axis_index("sector")
    me = lax.axis_index("blk")
    other = 1 - core
    z, x = me // 2, me % 2
    beside = me + 1 - 2 * x
    rank = me * 2 + core
    at_end = jnp.logical_or(z == 0, z == lines - 1)
    has = {DOWN: z > 0, UP: z < lines - 1, ACROSS: None}
    toward = {DOWN: me - 2, UP: me + 2, ACROSS: beside}

    wave_copy = pltpu.make_async_copy(wave_hbm, wave, local_sem.at[0])
    left_copy = pltpu.make_async_copy(
        left_hbm.at[0, :, 0], left.at[:, pl.ds(core * rows, rows)], local_sem.at[1]
    )
    right_copy = pltpu.make_async_copy(
        right_hbm.at[0, 0, pl.ds(core * half_cols, half_cols)], right.at[core], local_sem.at[2]
    )
    scalars = [(block_rows_hbm, block_rows), (pattern_hbm, pattern), (energy_hbm, energy)]
    scalar_copies = [
        pltpu.make_async_copy(source, target, local_sem.at[3 + index])
        for index, (source, target) in enumerate(scalars)
    ]

    barrier = pltpu.get_barrier_semaphore()
    def greet(block, which):
        pl.semaphore_signal(
            barrier,
            inc=1,
            device_id={"blk": block, "sector": which},
            device_id_type=pl.DeviceIdType.MESH,
        )

    greet(me, other)
    greet(beside, core)
    for way in (DOWN, UP):
        pl.when(has[way])(lambda: greet(toward[way], core))

    wave_copy.start()
    for copy in scalar_copies:
        copy.start()
    left_copy.start()
    right_copy.start()
    wave_copy.wait()
    for copy in scalar_copies:
        copy.wait()
    row_ids = lax.broadcasted_iota(jnp.int32, (rows, cols), 0)
    wave[...] = jnp.where(row_ids < block_rows[0], wave[...].astype(jnp.float32), 0.0).astype(
        wave.dtype
    )
    blocks[me] = wave[:, pl.ds(pl.multiple_of(core * half_cols, half_cols), half_cols)]
    pl.semaphore_wait(barrier, 2 + has[DOWN].astype(jnp.int32) + has[UP].astype(jnp.int32))

    sent = []

    def under(condition, action):
        if condition is None:
            action()
        else:
            pl.when(condition)(action)

    def both(first, second):
        if first is None:
            return second
        if second is None:
            return first
        return jnp.logical_and(first, second)

    def block_copy(block, piece, way):
        part = blocks.at[block, pl.ds(piece * half_rows, half_rows)]
        return pltpu.make_async_remote_copy(
            src_ref=part,
            dst_ref=part,
            send_sem=send_sem.at[block, piece, way],
            recv_sem=recv_sem.at[block, piece],
            device_id={"blk": toward[way], "sector": core},
            device_id_type=pl.DeviceIdType.MESH,
        )

    def send(block, piece, way, condition=None):
        condition = both(condition, has[way])
        under(condition, lambda: block_copy(block, piece, way).start())
        sent.append((block, piece, way, condition))

    def receive(block, piece, condition=None):
        under(condition, lambda: block_copy(block, piece, ACROSS).wait_recv())

    for piece in range(2):
        send(me, piece, DOWN)
        send(me, piece, UP)
        send(me, 1 - piece, ACROSS)

    def pair_copy(source, target, index):
        return pltpu.make_async_remote_copy(
            src_ref=source,
            dst_ref=target,
            send_sem=pair_send.at[index],
            recv_sem=pair_recv.at[index],
            device_id={"sector": other},
            device_id_type=pl.DeviceIdType.MESH,
        )

    left_copy.wait()
    for slot in range(n):
        mine = left[slot, pl.ds(core * rows, rows)].astype(jnp.float32)
        left[slot, pl.ds(core * rows, rows)] = (
            mine * pattern[slot].astype(jnp.float32)
        ).astype(left.dtype)
    own_left = left.at[:, pl.ds(core * rows, rows)]
    left_out = pair_copy(own_left, own_left, 0)
    left_out.start()
    right_out = pair_copy(
        right_hbm.at[0, 0, pl.ds(other * half_cols, half_cols)], right.at[core], 1
    )
    right_out.start()

    def accumulate(block, condition=None, fresh=False):
        def action():
            slot = lax.rem(block - me + middle + n, n)
            product = jnp.dot(left[slot], blocks[block], preferred_element_type=jnp.float32)
            acc[...] = product if fresh else acc[...] + product

        under(condition, action)

    def ends(distance):
        return (
            (beside + 2 * distance, z + distance == lines - 1, DOWN),
            (beside - 2 * distance, z == distance, UP),
        )

    def sides(block, distance):
        if distance == 0:
            return ((block, None, None),)
        return (
            (block + 2 * distance, z + distance < lines, DOWN),
            (block - 2 * distance, z >= distance, UP),
        )

    def forward(distance):
        for piece in range(2):
            for block, condition, way in sides(me, distance):
                receive(block, piece, condition)
                send(block, piece, way, condition)
                if piece == 0:
                    send(block, piece, ACROSS, condition)
            if piece == 1:
                for block, condition, way in sides(me, distance):
                    inner = both(condition, is_inner(distance, way))
                    send(block, piece, ACROSS, inner)
            if distance == 1 and piece == 0:
                receive(beside, 1)
                send(beside, 1, DOWN, at_end)
                send(beside, 1, UP, at_end)

    def is_inner(distance, way):
        return z + distance < lines - 1 if way == DOWN else z > distance

    def forward_ends(distance):
        for block, condition, way in ends(distance):
            receive(block, 1, condition)
            send(block, 1, way, condition)

    def own_line(distance):
        for block, condition, _ in sides(me, distance):
            accumulate(block, condition)

    def other_line(distance):
        for block, condition, way in sides(beside, distance):
            receive(block, 0, condition)
            if distance:
                receive(block, 1, both(condition, is_inner(distance, way)))
            accumulate(block, condition)

    for distance in range(1, lines):
        forward(distance)
        if distance < lines - 1:
            forward_ends(distance)
        if distance == 1:
            left_out.wait_recv()
            accumulate(me, fresh=True)
        else:
            other_line(distance - 2)
        own_line(distance)
    if lines > 1:
        other_line(lines - 2)
        forward_ends(lines - 1)
    else:
        left_out.wait_recv()
        accumulate(me, fresh=True)
        receive(beside, 1)
    other_line(lines - 1)

    right_copy.wait()
    right_out.wait_recv()

    wide = jnp.concatenate([acc[pl.ds(0, rows)], acc[pl.ds(rows, rows)]], axis=1)
    high = wide.astype(jnp.bfloat16)
    low = (wide - high.astype(jnp.float32)).astype(jnp.bfloat16)
    product = jnp.dot(
        jnp.concatenate([high, low], axis=0),
        right[...].reshape(cols, cols),
        preferred_element_type=jnp.float32,
    )
    partial[...] = product[:rows] + product[rows:]

    def lanes(values):
        summed = values[:, 0:128]
        for column in range(128, cols, 128):
            summed = summed + values[:, column : column + 128]
        return jnp.sum(summed, axis=0, keepdims=True)

    first_other = pl.multiple_of(other * half_rows, half_rows)
    first_own = pl.multiple_of(core * half_rows, half_rows)
    part_copy = pair_copy(partial.at[pl.ds(first_other, half_rows)], part_in, 2)
    part_copy.start()
    wave_own = wave[pl.ds(first_own, half_rows)].astype(jnp.float32)
    norm = lanes(wave_own * wave_own)
    correlation = lanes(partial[...] * wave[...].astype(jnp.float32)) + energy[0] * norm
    stat_rows = lax.broadcasted_iota(jnp.int32, (8, 128), 0)
    stats[rank] = jnp.where(stat_rows == 0, correlation, jnp.where(stat_rows == 1, norm, 0.0))

    def stat_copy(peer, slot):
        return pltpu.make_async_remote_copy(
            src_ref=stats.at[slot],
            dst_ref=stats.at[slot],
            send_sem=stat_send.at[peer],
            recv_sem=stat_recv.at[slot],
            device_id={"blk": peer // 2, "sector": peer % 2},
            device_id_type=pl.DeviceIdType.MESH,
        )

    turn = 1 - 2 * (z < lines // 2).astype(jnp.int32)
    peers = []
    for step in range(lines):
        line = lax.rem(lines - 1 - z + step * turn + lines * lines, lines)
        peers += [line * 4 + place for place in range(4)]
    for peer in peers:
        pl.when(peer != rank)(lambda: stat_copy(peer, rank).start())

    part_copy.wait_recv()
    live = lax.broadcasted_iota(jnp.int32, (half_rows, cols), 0) + first_own < block_rows[0]
    sigma = jnp.where(
        live,
        partial[pl.ds(first_own, half_rows)] + part_in[...] + energy[0] * wave_own,
        0.0,
    )
    part_in[...] = sigma
    for peer in range(2 * n):
        pl.when(peer != rank)(lambda: stat_copy(peer, peer).wait_recv())
    total = jnp.sum(stats[...], axis=0)
    totals = jnp.sum(total, axis=1, keepdims=True)
    quotient = totals[0:1] / totals[1:2]
    rayleigh[0] = quotient[0, 0]
    residual[...] = part_in[...] - quotient * wave_own

    for block, piece, way, condition in sent:
        under(condition, lambda: block_copy(block, piece, way).wait_send())
    left_out.wait_send()
    right_out.wait_send()
    part_copy.wait_send()
    for peer in range(2 * n):
        pl.when(peer != rank)(lambda: stat_copy(peer, rank).wait_send())


def line_shards(wavefunction, env_left, pattern, env_right, energy, block_rows):
    n = lax.axis_size("blk")
    rows, cols = wavefunction.shape
    half_rows, half_cols = rows // 2, cols // 2
    bf16, f32 = jnp.bfloat16, jnp.float32
    dma = pltpu.SemaphoreType.DMA
    smem = pl.BlockSpec(memory_space=pltpu.SMEM)
    hbm = pl.BlockSpec(memory_space=pl.ANY)
    residual, rayleigh = pl.pallas_call(
        functools.partial(kernel, n),
        out_shape=(
            jax.ShapeDtypeStruct((half_rows, cols), f32),
            jax.ShapeDtypeStruct((1,), f32),
        ),
        in_specs=[hbm] * 6,
        out_specs=(pl.BlockSpec(memory_space=pltpu.VMEM), smem),
        scratch_shapes=[
            pltpu.SMEM((n,), jnp.int32),
            pltpu.SMEM((1,), f32),
            pltpu.SMEM((1,), jnp.int32),
            pltpu.VMEM((rows, cols), bf16),
            pltpu.VMEM((n, rows, half_cols), bf16),
            pltpu.VMEM((n, 2 * rows, rows), bf16),
            pltpu.VMEM((2, half_cols, cols), bf16),
            pltpu.VMEM((2 * rows, half_cols), f32),
            pltpu.VMEM((rows, cols), f32),
            pltpu.VMEM((half_rows, cols), f32),
            pltpu.VMEM((2 * n, 8, 128), f32),
            dma((6,)),
            dma((n, 2, 3)),
            dma((n, 2)),
            dma((3,)),
            dma((3,)),
            dma((2 * n,)),
            dma((2 * n,)),
        ],
        compiler_params=pltpu.CompilerParams(
            collective_id=0, has_side_effects=True, vmem_limit_bytes=(53 * 1024 + 512) * 1024
        ),
        cost_estimate=pl.CostEstimate(
            flops=6 * rows * rows * cols * n, bytes_accessed=4 * n * rows * rows, transcendentals=0
        ),
    )(wavefunction, env_left, env_right, pattern.reshape(n), energy, block_rows)
    return residual, rayleigh


def solution(mesh):
    blk = mesh.shape["blk"]

    def shards(wavefunction, env_left, pattern, env_right, energy, block_rows):
        all_coupled = env_left.shape[1] == blk and blk % 2 == 0
        body = line_shards if all_coupled else ring_shards
        return body(wavefunction, env_left, pattern, env_right, energy, block_rows)

    return jax.shard_map(
        shards,
        mesh=mesh,
        in_specs=(
            P(("groups", "blk"), None),
            P(("groups", "blk"), None, "sector", None, None),
            P(("groups", "blk"), None, "sector"),
            P(("groups", "blk"), "sector", None, None),
            P(("groups", "blk")),
            P(("groups", "blk")),
        ),
        out_specs=(P(("groups", "blk", "sector"), None), P("groups")),
        check_vma=False,
    )
```

```python
import functools

import jax
import jax.numpy as jnp
from jax import lax
from jax.experimental import pallas as pl
from jax.experimental.pallas import tpu as pltpu
from jax.sharding import PartitionSpec as P

DOWN, UP, ACROSS = 0, 1, 2
CUTS = 2


def from_behind(value, axis, steps):
    count = lax.axis_size(axis)
    pairs = [(source, (source + steps) % count) for source in range(count)]
    return lax.ppermute(value, axis, pairs)


def ring_shards(wavefunction, env_left, pattern, env_right, energy, block_rows):
    rows_pad = env_left.shape[-1]
    loop_len = env_left.shape[1]
    middle = loop_len // 2
    half_rows = rows_pad // 2
    live_rows = (jnp.arange(rows_pad) < block_rows[0]).astype(jnp.bfloat16)
    own_block = wavefunction * live_rows[:, None]
    coupled = env_left[0, :, 0] * pattern[0, :, 0].astype(jnp.bfloat16)[:, None, None]
    core_index = lax.axis_index("sector")
    own_half = lax.dynamic_slice_in_dim(own_block, core_index * half_rows, half_rows, 0)

    def add_term(summed_now, slot, pieces):
        term_env = lax.dynamic_index_in_dim(coupled, slot, 0, keepdims=False)
        return summed_now + jnp.dot(term_env, pieces, preferred_element_type=jnp.float32)

    moving = from_behind(own_block, "blk", middle)
    summed = jnp.zeros((rows_pad, own_block.shape[1]), jnp.float32)
    summed = add_term(summed, 0, moving)

    def advance(turn, state):
        moving_now, summed_now = state
        moving_now = from_behind(moving_now, "blk", -1)
        return (moving_now, add_term(summed_now, turn, moving_now))

    moving, summed = lax.fori_loop(1, loop_len, advance, (moving, summed))
    partial_sigma = jnp.dot(
        summed,
        env_right[0, 0].astype(jnp.float32),
        precision=lax.Precision.HIGHEST,
        preferred_element_type=jnp.float32,
    )
    summed_terms = lax.psum(partial_sigma, "sector")
    mine = lax.dynamic_slice_in_dim(summed_terms, core_index * half_rows, half_rows, 0)
    live_half = lax.dynamic_slice_in_dim(live_rows, core_index * half_rows, half_rows, 0).astype(
        jnp.float32
    )
    own_wide = own_half.astype(jnp.float32)
    sigma_half = (mine + energy[0] * own_wide) * live_half[:, None]
    correlation, norm_sq = lax.psum(
        (jnp.sum(own_wide * sigma_half), jnp.sum(own_wide * own_wide)), ("blk", "sector")
    )
    rayleigh = correlation / norm_sq
    residual = sigma_half - rayleigh * own_wide
    return (residual, rayleigh.reshape(1))


def kernel(
    n,
    wave_hbm,
    left_hbm,
    right_hbm,
    pattern_hbm,
    energy_hbm,
    block_rows_hbm,
    residual,
    rayleigh,
    pattern,
    energy,
    block_rows,
    wave,
    blocks,
    left,
    right,
    acc,
    partial,
    part_in,
    stats,
    local_sem,
    send_sem,
    recv_sem,
    pair_send,
    pair_recv,
    stat_send,
    stat_recv,
):
    lines = n // 2
    rows, cols = wave.shape
    half_rows, half_cols = rows // 2, cols // 2
    piece_rows = half_rows // CUTS
    halves = (range(CUTS), range(CUTS, 2 * CUTS))
    middle = n // 2
    core = lax.axis_index("sector")
    me = lax.axis_index("blk")
    other = 1 - core
    z, x = me // 2, me % 2
    beside = me + 1 - 2 * x
    rank = me * 2 + core
    at_end = jnp.logical_or(z == 0, z == lines - 1)
    has = {DOWN: z > 0, UP: z < lines - 1, ACROSS: None}
    toward = {DOWN: me - 2, UP: me + 2, ACROSS: beside}

    wave_copy = pltpu.make_async_copy(wave_hbm, wave, local_sem.at[0])
    left_copy = pltpu.make_async_copy(
        left_hbm.at[0, :, 0], left.at[:, pl.ds(core * rows, rows)], local_sem.at[1]
    )
    right_copy = pltpu.make_async_copy(
        right_hbm.at[0, 0, pl.ds(core * half_cols, half_cols)], right.at[core], local_sem.at[2]
    )
    scalars = [(block_rows_hbm, block_rows), (pattern_hbm, pattern), (energy_hbm, energy)]
    scalar_copies = [
        pltpu.make_async_copy(source, target, local_sem.at[3 + index])
        for index, (source, target) in enumerate(scalars)
    ]

    barrier = pltpu.get_barrier_semaphore()
    def greet(block, which):
        pl.semaphore_signal(
            barrier,
            inc=1,
            device_id={"blk": block, "sector": which},
            device_id_type=pl.DeviceIdType.MESH,
        )

    greet(me, other)
    greet(beside, core)
    for way in (DOWN, UP):
        pl.when(has[way])(lambda: greet(toward[way], core))

    wave_copy.start()
    for copy in scalar_copies:
        copy.start()
    left_copy.start()
    right_copy.start()
    wave_copy.wait()
    for copy in scalar_copies:
        copy.wait()
    row_ids = lax.broadcasted_iota(jnp.int32, (rows, cols), 0)
    wave[...] = jnp.where(row_ids < block_rows[0], wave[...].astype(jnp.float32), 0.0).astype(
        wave.dtype
    )
    blocks[me] = wave[:, pl.ds(pl.multiple_of(core * half_cols, half_cols), half_cols)]
    pl.semaphore_wait(barrier, 2 + has[DOWN].astype(jnp.int32) + has[UP].astype(jnp.int32))

    sent = []

    def under(condition, action):
        if condition is None:
            action()
        else:
            pl.when(condition)(action)

    def both(first, second):
        if first is None:
            return second
        if second is None:
            return first
        return jnp.logical_and(first, second)

    def block_copy(block, piece, way):
        part = blocks.at[block, pl.ds(piece * piece_rows, piece_rows)]
        return pltpu.make_async_remote_copy(
            src_ref=part,
            dst_ref=part,
            send_sem=send_sem.at[block, piece, way],
            recv_sem=recv_sem.at[block, piece],
            device_id={"blk": toward[way], "sector": core},
            device_id_type=pl.DeviceIdType.MESH,
        )

    def send(block, piece, way, condition=None):
        condition = both(condition, has[way])
        under(condition, lambda: block_copy(block, piece, way).start())
        sent.append((block, piece, way, condition))

    def receive(block, piece, condition=None):
        under(condition, lambda: block_copy(block, piece, ACROSS).wait_recv())

    for piece in range(2 * CUTS):
        send(me, (piece + CUTS) % (2 * CUTS), ACROSS)
        send(me, piece, DOWN)
        send(me, piece, UP)

    def pair_copy(source, target, index):
        return pltpu.make_async_remote_copy(
            src_ref=source,
            dst_ref=target,
            send_sem=pair_send.at[index],
            recv_sem=pair_recv.at[index],
            device_id={"sector": other},
            device_id_type=pl.DeviceIdType.MESH,
        )

    left_copy.wait()
    for slot in range(n):
        mine = left[slot, pl.ds(core * rows, rows)].astype(jnp.float32)
        left[slot, pl.ds(core * rows, rows)] = (
            mine * pattern[slot].astype(jnp.float32)
        ).astype(left.dtype)
    own_left = left.at[:, pl.ds(core * rows, rows)]
    left_out = pair_copy(own_left, own_left, 0)
    left_out.start()
    right_out = pair_copy(
        right_hbm.at[0, 0, pl.ds(other * half_cols, half_cols)], right.at[core], 1
    )
    right_out.start()

    def accumulate(block, condition=None, fresh=False):
        def action():
            slot = lax.rem(block - me + middle + n, n)
            product = jnp.dot(left[slot], blocks[block], preferred_element_type=jnp.float32)
            acc[...] = product if fresh else acc[...] + product

        under(condition, action)

    def ends(distance):
        return (
            (beside + 2 * distance, z + distance == lines - 1, DOWN),
            (beside - 2 * distance, z == distance, UP),
        )

    def sides(block, distance):
        if distance == 0:
            return ((block, None, None),)
        return (
            (block + 2 * distance, z + distance < lines, DOWN),
            (block - 2 * distance, z >= distance, UP),
        )

    def forward(distance):
        for piece in halves[0]:
            for block, condition, way in sides(me, distance):
                receive(block, piece, condition)
                send(block, piece, way, condition)
                send(block, piece, ACROSS, condition)
        if distance == 1:
            for piece in halves[1]:
                receive(beside, piece)
                send(beside, piece, DOWN, at_end)
                send(beside, piece, UP, at_end)
        for piece in halves[1]:
            for block, condition, way in sides(me, distance):
                receive(block, piece, condition)
                send(block, piece, way, condition)
            for block, condition, way in sides(me, distance):
                send(block, piece, ACROSS, both(condition, is_inner(distance, way)))

    def is_inner(distance, way):
        return z + distance < lines - 1 if way == DOWN else z > distance

    def forward_ends(distance):
        for piece in halves[1]:
            for block, condition, way in ends(distance):
                receive(block, piece, condition)
                send(block, piece, way, condition)

    def own_line(distance):
        for block, condition, _ in sides(me, distance):
            accumulate(block, condition)

    def other_line(distance):
        for block, condition, way in sides(beside, distance):
            for piece in halves[0]:
                receive(block, piece, condition)
            if distance:
                for piece in halves[1]:
                    receive(block, piece, both(condition, is_inner(distance, way)))
            accumulate(block, condition)

    for distance in range(1, lines):
        forward(distance)
        if distance < lines - 1:
            forward_ends(distance)
        if distance == 1:
            left_out.wait_recv()
            accumulate(me, fresh=True)
        else:
            other_line(distance - 2)
        own_line(distance)
    if lines > 1:
        other_line(lines - 2)
        forward_ends(lines - 1)
    else:
        left_out.wait_recv()
        accumulate(me, fresh=True)
        for piece in halves[1]:
            receive(beside, piece)
    other_line(lines - 1)

    right_copy.wait()
    right_out.wait_recv()

    wide = jnp.concatenate([acc[pl.ds(0, rows)], acc[pl.ds(rows, rows)]], axis=1)
    high = wide.astype(jnp.bfloat16)
    low = (wide - high.astype(jnp.float32)).astype(jnp.bfloat16)
    product = jnp.dot(
        jnp.concatenate([high, low], axis=0),
        right[...].reshape(cols, cols),
        preferred_element_type=jnp.float32,
    )
    partial[...] = product[:rows] + product[rows:]

    def lanes(values):
        summed = values[:, 0:128]
        for column in range(128, cols, 128):
            summed = summed + values[:, column : column + 128]
        return jnp.sum(summed, axis=0, keepdims=True)

    first_other = pl.multiple_of(other * half_rows, half_rows)
    first_own = pl.multiple_of(core * half_rows, half_rows)
    part_copy = pair_copy(partial.at[pl.ds(first_other, half_rows)], part_in, 2)
    part_copy.start()
    wave_own = wave[pl.ds(first_own, half_rows)].astype(jnp.float32)
    norm = lanes(wave_own * wave_own)
    correlation = lanes(partial[...] * wave[...].astype(jnp.float32)) + energy[0] * norm
    stat_rows = lax.broadcasted_iota(jnp.int32, (8, 128), 0)
    stats[rank] = jnp.where(stat_rows == 0, correlation, jnp.where(stat_rows == 1, norm, 0.0))

    def stat_copy(peer, slot):
        return pltpu.make_async_remote_copy(
            src_ref=stats.at[slot],
            dst_ref=stats.at[slot],
            send_sem=stat_send.at[peer],
            recv_sem=stat_recv.at[slot],
            device_id={"blk": peer // 2, "sector": peer % 2},
            device_id_type=pl.DeviceIdType.MESH,
        )

    turn = 1 - 2 * (z < lines // 2).astype(jnp.int32)
    peers = []
    for step in range(lines):
        line = lax.rem(lines - 1 - z + step * turn + lines * lines, lines)
        peers += [line * 4 + place for place in range(4)]
    for peer in peers:
        pl.when(peer != rank)(lambda: stat_copy(peer, rank).start())

    part_copy.wait_recv()
    live = lax.broadcasted_iota(jnp.int32, (half_rows, cols), 0) + first_own < block_rows[0]
    sigma = jnp.where(
        live,
        partial[pl.ds(first_own, half_rows)] + part_in[...] + energy[0] * wave_own,
        0.0,
    )
    part_in[...] = sigma
    for block, piece, way, condition in sent:
        under(condition, lambda: block_copy(block, piece, way).wait_send())
    left_out.wait_send()
    right_out.wait_send()
    part_copy.wait_send()
    for peer in range(2 * n):
        pl.when(peer != rank)(lambda: stat_copy(peer, rank).wait_send())
    for peer in range(2 * n):
        pl.when(peer != rank)(lambda: stat_copy(peer, peer).wait_recv())
    total = jnp.sum(stats[...], axis=0)
    totals = jnp.sum(total, axis=1, keepdims=True)
    quotient = totals[0:1] / totals[1:2]
    rayleigh[0] = quotient[0, 0]
    residual[...] = part_in[...] - quotient * wave_own


def line_shards(wavefunction, env_left, pattern, env_right, energy, block_rows):
    n = lax.axis_size("blk")
    rows, cols = wavefunction.shape
    half_rows, half_cols = rows // 2, cols // 2
    bf16, f32 = jnp.bfloat16, jnp.float32
    dma = pltpu.SemaphoreType.DMA
    smem = pl.BlockSpec(memory_space=pltpu.SMEM)
    hbm = pl.BlockSpec(memory_space=pl.ANY)
    residual, rayleigh = pl.pallas_call(
        functools.partial(kernel, n),
        out_shape=(
            jax.ShapeDtypeStruct((half_rows, cols), f32),
            jax.ShapeDtypeStruct((1,), f32),
        ),
        in_specs=[hbm] * 6,
        out_specs=(pl.BlockSpec(memory_space=pltpu.VMEM), smem),
        scratch_shapes=[
            pltpu.SMEM((n,), jnp.int32),
            pltpu.SMEM((1,), f32),
            pltpu.SMEM((1,), jnp.int32),
            pltpu.VMEM((rows, cols), bf16),
            pltpu.VMEM((n, rows, half_cols), bf16),
            pltpu.VMEM((n, 2 * rows, rows), bf16),
            pltpu.VMEM((2, half_cols, cols), bf16),
            pltpu.VMEM((2 * rows, half_cols), f32),
            pltpu.VMEM((rows, cols), f32),
            pltpu.VMEM((half_rows, cols), f32),
            pltpu.VMEM((2 * n, 8, 128), f32),
            dma((6,)),
            dma((n, 2 * CUTS, 3)),
            dma((n, 2 * CUTS)),
            dma((3,)),
            dma((3,)),
            dma((2 * n,)),
            dma((2 * n,)),
        ],
        compiler_params=pltpu.CompilerParams(
            collective_id=0, has_side_effects=True, vmem_limit_bytes=(53 * 1024 + 512) * 1024
        ),
        cost_estimate=pl.CostEstimate(
            flops=6 * rows * rows * cols * n, bytes_accessed=4 * n * rows * rows, transcendentals=0
        ),
    )(wavefunction, env_left, env_right, pattern.reshape(n), energy, block_rows)
    return residual, rayleigh


def solution(mesh):
    blk = mesh.shape["blk"]

    def shards(wavefunction, env_left, pattern, env_right, energy, block_rows):
        all_coupled = env_left.shape[1] == blk and blk % 2 == 0
        body = line_shards if all_coupled else ring_shards
        return body(wavefunction, env_left, pattern, env_right, energy, block_rows)

    return jax.shard_map(
        shards,
        mesh=mesh,
        in_specs=(
            P(("groups", "blk"), None),
            P(("groups", "blk"), None, "sector", None, None),
            P(("groups", "blk"), None, "sector"),
            P(("groups", "blk"), "sector", None, None),
            P(("groups", "blk")),
            P(("groups", "blk")),
        ),
        out_specs=(P(("groups", "blk", "sector"), None), P("groups")),
        check_vma=False,
    )
```

```python
import functools

import jax
import jax.numpy as jnp
from jax import lax
from jax.experimental import pallas as pl
from jax.experimental.pallas import tpu as pltpu
from jax.sharding import PartitionSpec as P

DOWN, UP, ACROSS = 0, 1, 2
CUTS = 2


def from_behind(value, axis, steps):
    count = lax.axis_size(axis)
    pairs = [(source, (source + steps) % count) for source in range(count)]
    return lax.ppermute(value, axis, pairs)


def ring_shards(wavefunction, env_left, pattern, env_right, energy, block_rows):
    rows_pad = env_left.shape[-1]
    loop_len = env_left.shape[1]
    middle = loop_len // 2
    half_rows = rows_pad // 2
    live_rows = (jnp.arange(rows_pad) < block_rows[0]).astype(jnp.bfloat16)
    own_block = wavefunction * live_rows[:, None]
    coupled = env_left[0, :, 0] * pattern[0, :, 0].astype(jnp.bfloat16)[:, None, None]
    core_index = lax.axis_index("sector")
    own_half = lax.dynamic_slice_in_dim(own_block, core_index * half_rows, half_rows, 0)

    def add_term(summed_now, slot, pieces):
        term_env = lax.dynamic_index_in_dim(coupled, slot, 0, keepdims=False)
        return summed_now + jnp.dot(term_env, pieces, preferred_element_type=jnp.float32)

    moving = from_behind(own_block, "blk", middle)
    summed = jnp.zeros((rows_pad, own_block.shape[1]), jnp.float32)
    summed = add_term(summed, 0, moving)

    def advance(turn, state):
        moving_now, summed_now = state
        moving_now = from_behind(moving_now, "blk", -1)
        return (moving_now, add_term(summed_now, turn, moving_now))

    moving, summed = lax.fori_loop(1, loop_len, advance, (moving, summed))
    partial_sigma = jnp.dot(
        summed,
        env_right[0, 0].astype(jnp.float32),
        precision=lax.Precision.HIGHEST,
        preferred_element_type=jnp.float32,
    )
    summed_terms = lax.psum(partial_sigma, "sector")
    mine = lax.dynamic_slice_in_dim(summed_terms, core_index * half_rows, half_rows, 0)
    live_half = lax.dynamic_slice_in_dim(live_rows, core_index * half_rows, half_rows, 0).astype(
        jnp.float32
    )
    own_wide = own_half.astype(jnp.float32)
    sigma_half = (mine + energy[0] * own_wide) * live_half[:, None]
    correlation, norm_sq = lax.psum(
        (jnp.sum(own_wide * sigma_half), jnp.sum(own_wide * own_wide)), ("blk", "sector")
    )
    rayleigh = correlation / norm_sq
    residual = sigma_half - rayleigh * own_wide
    return (residual, rayleigh.reshape(1))


def kernel(
    n,
    wave_hbm,
    left_hbm,
    right_hbm,
    pattern_hbm,
    energy_hbm,
    block_rows_hbm,
    residual,
    rayleigh,
    pattern,
    energy,
    block_rows,
    wave,
    blocks,
    left,
    right,
    acc,
    partial,
    part_in,
    weights,
    tall_both,
    bilinear,
    stats,
    local_sem,
    send_sem,
    recv_sem,
    pair_send,
    pair_recv,
    stat_send,
    stat_recv,
):
    lines = n // 2
    rows, cols = wave.shape
    half_rows, half_cols = rows // 2, cols // 2
    piece_rows = half_rows // CUTS
    halves = (range(CUTS), range(CUTS, 2 * CUTS))
    middle = n // 2
    core = lax.axis_index("sector")
    me = lax.axis_index("blk")
    other = 1 - core
    z, x = me // 2, me % 2
    beside = me + 1 - 2 * x
    rank = me * 2 + core
    at_end = jnp.logical_or(z == 0, z == lines - 1)
    has = {DOWN: z > 0, UP: z < lines - 1, ACROSS: None}
    toward = {DOWN: me - 2, UP: me + 2, ACROSS: beside}

    wave_copy = pltpu.make_async_copy(wave_hbm, wave, local_sem.at[0])
    left_copy = pltpu.make_async_copy(
        left_hbm.at[0, :, 0], left.at[:, pl.ds(core * rows, rows)], local_sem.at[1]
    )
    right_copy = pltpu.make_async_copy(
        right_hbm.at[0, 0, pl.ds(core * half_cols, half_cols)], right.at[core], local_sem.at[2]
    )
    scalars = [(block_rows_hbm, block_rows), (pattern_hbm, pattern), (energy_hbm, energy)]
    scalar_copies = [
        pltpu.make_async_copy(source, target, local_sem.at[3 + index])
        for index, (source, target) in enumerate(scalars)
    ]

    barrier = pltpu.get_barrier_semaphore()
    def greet(block, which):
        pl.semaphore_signal(
            barrier,
            inc=1,
            device_id={"blk": block, "sector": which},
            device_id_type=pl.DeviceIdType.MESH,
        )

    greet(me, other)
    greet(beside, core)
    for way in (DOWN, UP):
        pl.when(has[way])(lambda: greet(toward[way], core))

    wave_copy.start()
    for copy in scalar_copies:
        copy.start()
    left_copy.start()
    right_copy.start()
    wave_copy.wait()
    for copy in scalar_copies:
        copy.wait()
    row_ids = lax.broadcasted_iota(jnp.int32, (rows, cols), 0)
    wave[...] = jnp.where(row_ids < block_rows[0], wave[...].astype(jnp.float32), 0.0).astype(
        wave.dtype
    )
    blocks[me] = wave[:, pl.ds(pl.multiple_of(core * half_cols, half_cols), half_cols)]
    pl.semaphore_wait(barrier, 2 + has[DOWN].astype(jnp.int32) + has[UP].astype(jnp.int32))

    sent = []

    def under(condition, action):
        if condition is None:
            action()
        else:
            pl.when(condition)(action)

    def both(first, second):
        if first is None:
            return second
        if second is None:
            return first
        return jnp.logical_and(first, second)

    def block_copy(block, piece, way):
        part = blocks.at[block, pl.ds(piece * piece_rows, piece_rows)]
        return pltpu.make_async_remote_copy(
            src_ref=part,
            dst_ref=part,
            send_sem=send_sem.at[block, piece, way],
            recv_sem=recv_sem.at[block, piece],
            device_id={"blk": toward[way], "sector": core},
            device_id_type=pl.DeviceIdType.MESH,
        )

    def send(block, piece, way, condition=None):
        condition = both(condition, has[way])
        under(condition, lambda: block_copy(block, piece, way).start())
        sent.append((block, piece, way, condition))

    def receive(block, piece, condition=None):
        under(condition, lambda: block_copy(block, piece, ACROSS).wait_recv())

    for piece in range(2 * CUTS):
        send(me, (piece + CUTS) % (2 * CUTS), ACROSS)
        send(me, piece, DOWN)
        send(me, piece, UP)

    def pair_copy(source, target, index):
        return pltpu.make_async_remote_copy(
            src_ref=source,
            dst_ref=target,
            send_sem=pair_send.at[index],
            recv_sem=pair_recv.at[index],
            device_id={"sector": other},
            device_id_type=pl.DeviceIdType.MESH,
        )

    left_copy.wait()
    for slot in range(n):
        mine = left[slot, pl.ds(core * rows, rows)].astype(jnp.float32)
        left[slot, pl.ds(core * rows, rows)] = (
            mine * pattern[slot].astype(jnp.float32)
        ).astype(left.dtype)
    own_left = left.at[:, pl.ds(core * rows, rows)]
    left_out = pair_copy(own_left, own_left, 0)
    left_out.start()
    right_out = pair_copy(
        right_hbm.at[0, 0, pl.ds(other * half_cols, half_cols)], right.at[core], 1
    )
    right_out.start()

    def accumulate(block, condition=None, fresh=False):
        def action():
            slot = lax.rem(block - me + middle + n, n)
            product = jnp.dot(left[slot], blocks[block], preferred_element_type=jnp.float32)
            acc[...] = product if fresh else acc[...] + product
            met = weights[slot] * blocks[block].astype(jnp.float32)
            met = jnp.sum(met.reshape(rows // 8, 8, half_cols), axis=0)
            bilinear[...] = met if fresh else bilinear[...] + met

        under(condition, action)

    def ends(distance):
        return (
            (beside + 2 * distance, z + distance == lines - 1, DOWN),
            (beside - 2 * distance, z == distance, UP),
        )

    def sides(block, distance):
        if distance == 0:
            return ((block, None, None),)
        return (
            (block + 2 * distance, z + distance < lines, DOWN),
            (block - 2 * distance, z >= distance, UP),
        )

    def forward(distance, between=lambda: None):
        for piece in halves[0]:
            for block, condition, way in sides(me, distance):
                receive(block, piece, condition)
                send(block, piece, way, condition)
                send(block, piece, ACROSS, condition)
            between()
        if distance == 1:
            for piece in halves[1]:
                receive(beside, piece)
                send(beside, piece, DOWN, at_end)
                send(beside, piece, UP, at_end)
        for piece in halves[1]:
            for block, condition, way in sides(me, distance):
                receive(block, piece, condition)
                send(block, piece, way, condition)
            for block, condition, way in sides(me, distance):
                send(block, piece, ACROSS, both(condition, is_inner(distance, way)))
            between()

    def is_inner(distance, way):
        return z + distance < lines - 1 if way == DOWN else z > distance

    def forward_ends(distance):
        for piece in halves[1]:
            for block, condition, way in ends(distance):
                receive(block, piece, condition)
                send(block, piece, way, condition)

    def own_line(distance):
        for block, condition, _ in sides(me, distance):
            accumulate(block, condition)

    def other_line(distance):
        for block, condition, way in sides(beside, distance):
            for piece in halves[0]:
                receive(block, piece, condition)
            if distance:
                for piece in halves[1]:
                    receive(block, piece, both(condition, is_inner(distance, way)))
            accumulate(block, condition)

    def weigh():
        left_out.wait_recv()
        right_copy.wait()
        right_out.wait_recv()
        sides_two = []
        for term in range(2):
            sides_two.append(
                lax.dot_general(
                    wave[...],
                    right[term],
                    (((1,), (1,)), ((), ())),
                    preferred_element_type=jnp.float32,
                )
            )
        tall = jnp.concatenate(sides_two, axis=0)
        tall_high = tall.astype(jnp.bfloat16)
        tall_low = (tall - tall_high.astype(jnp.float32)).astype(jnp.bfloat16)
        tall_both[...] = jnp.concatenate([tall_high, tall_low], axis=1)

    def weigh_slots(first, last):
        def one(slot, carry):
            product = lax.dot_general(
                left[slot],
                tall_both[...],
                (((0,), (0,)), ((), ())),
                preferred_element_type=jnp.float32,
            )
            weights[slot] = product[:, :half_cols] + product[:, half_cols:]
            return carry

        lax.fori_loop(first, last, one, 0)

    todo = list(range(n))

    def next_slots():
        if todo:
            weigh_slots(todo[0], todo[0] + 2)
            del todo[:2]

    for distance in range(1, lines):
        forward(distance, next_slots if distance == 2 else lambda: None)
        if distance < lines - 1:
            forward_ends(distance)
        if distance == 1:
            weigh()
        else:
            while todo:
                next_slots()
            if distance == 2:
                accumulate(me, fresh=True)
                own_line(1)
            other_line(distance - 2)
            own_line(distance)
    other_line(lines - 2)
    forward_ends(lines - 1)
    other_line(lines - 1)

    def lanes(values):
        summed = values[:, 0:128]
        for column in range(128, values.shape[1], 128):
            summed = summed + values[:, column : column + 128]
        return jnp.sum(summed, axis=0, keepdims=True)

    first_other = pl.multiple_of(other * half_rows, half_rows)
    first_own = pl.multiple_of(core * half_rows, half_rows)
    wave_own = wave[pl.ds(first_own, half_rows)].astype(jnp.float32)
    norm = lanes(wave_own * wave_own)
    correlation = lanes(bilinear[...]) + energy[0] * norm
    stat_rows = lax.broadcasted_iota(jnp.int32, (8, 128), 0)
    stats[rank] = jnp.where(stat_rows == 0, correlation, jnp.where(stat_rows == 1, norm, 0.0))

    def stat_copy(peer, slot):
        return pltpu.make_async_remote_copy(
            src_ref=stats.at[slot],
            dst_ref=stats.at[slot],
            send_sem=stat_send.at[peer],
            recv_sem=stat_recv.at[slot],
            device_id={"blk": peer // 2, "sector": peer % 2},
            device_id_type=pl.DeviceIdType.MESH,
        )

    turn = 1 - 2 * (z < lines // 2).astype(jnp.int32)
    peers = []
    for step in range(lines):
        line = lax.rem(lines - 1 - z + step * turn + lines * lines, lines)
        peers += [line * 4 + place for place in range(4)]
    for peer in peers:
        pl.when(peer != rank)(lambda: stat_copy(peer, rank).start())

    wide = jnp.concatenate([acc[pl.ds(0, rows)], acc[pl.ds(rows, rows)]], axis=1)
    high = wide.astype(jnp.bfloat16)
    low = (wide - high.astype(jnp.float32)).astype(jnp.bfloat16)
    product = jnp.dot(
        jnp.concatenate([high, low], axis=0),
        right[...].reshape(cols, cols),
        preferred_element_type=jnp.float32,
    )
    partial[...] = product[:rows] + product[rows:]

    part_copy = pair_copy(partial.at[pl.ds(first_other, half_rows)], part_in, 2)
    part_copy.start()
    part_copy.wait_recv()
    live = lax.broadcasted_iota(jnp.int32, (half_rows, cols), 0) + first_own < block_rows[0]
    sigma = jnp.where(
        live,
        partial[pl.ds(first_own, half_rows)] + part_in[...] + energy[0] * wave_own,
        0.0,
    )
    part_in[...] = sigma
    for block, piece, way, condition in sent:
        under(condition, lambda: block_copy(block, piece, way).wait_send())
    left_out.wait_send()
    right_out.wait_send()
    part_copy.wait_send()
    for peer in range(2 * n):
        pl.when(peer != rank)(lambda: stat_copy(peer, rank).wait_send())
    for peer in range(2 * n):
        pl.when(peer != rank)(lambda: stat_copy(peer, peer).wait_recv())
    total = jnp.sum(stats[...], axis=0)
    totals = jnp.sum(total, axis=1, keepdims=True)
    quotient = totals[0:1] / totals[1:2]
    rayleigh[0] = quotient[0, 0]
    residual[...] = part_in[...] - quotient * wave_own


def line_shards(wavefunction, env_left, pattern, env_right, energy, block_rows):
    n = lax.axis_size("blk")
    rows, cols = wavefunction.shape
    half_rows, half_cols = rows // 2, cols // 2
    bf16, f32 = jnp.bfloat16, jnp.float32
    dma = pltpu.SemaphoreType.DMA
    smem = pl.BlockSpec(memory_space=pltpu.SMEM)
    hbm = pl.BlockSpec(memory_space=pl.ANY)
    residual, rayleigh = pl.pallas_call(
        functools.partial(kernel, n),
        out_shape=(
            jax.ShapeDtypeStruct((half_rows, cols), f32),
            jax.ShapeDtypeStruct((1,), f32),
        ),
        in_specs=[hbm] * 6,
        out_specs=(pl.BlockSpec(memory_space=pltpu.VMEM), smem),
        scratch_shapes=[
            pltpu.SMEM((n,), jnp.int32),
            pltpu.SMEM((1,), f32),
            pltpu.SMEM((1,), jnp.int32),
            pltpu.VMEM((rows, cols), bf16),
            pltpu.VMEM((n, rows, half_cols), bf16),
            pltpu.VMEM((n, 2 * rows, rows), bf16),
            pltpu.VMEM((2, half_cols, cols), bf16),
            pltpu.VMEM((2 * rows, half_cols), f32),
            pltpu.VMEM((rows, cols), f32),
            pltpu.VMEM((half_rows, cols), f32),
            pltpu.VMEM((n, rows, half_cols), f32),
            pltpu.VMEM((2 * rows, cols), bf16),
            pltpu.VMEM((8, half_cols), f32),
            pltpu.VMEM((2 * n, 8, 128), f32),
            dma((6,)),
            dma((n, 2 * CUTS, 3)),
            dma((n, 2 * CUTS)),
            dma((3,)),
            dma((3,)),
            dma((2 * n,)),
            dma((2 * n,)),
        ],
        compiler_params=pltpu.CompilerParams(
            collective_id=0, has_side_effects=True, vmem_limit_bytes=(53 * 1024 + 512) * 1024
        ),
        cost_estimate=pl.CostEstimate(
            flops=6 * rows * rows * cols * n, bytes_accessed=4 * n * rows * rows, transcendentals=0
        ),
    )(wavefunction, env_left, env_right, pattern.reshape(n), energy, block_rows)
    return residual, rayleigh


def solution(mesh):
    blk = mesh.shape["blk"]

    def shards(wavefunction, env_left, pattern, env_right, energy, block_rows):
        all_coupled = env_left.shape[1] == blk and blk % 2 == 0 and blk >= 6
        body = line_shards if all_coupled else ring_shards
        return body(wavefunction, env_left, pattern, env_right, energy, block_rows)

    return jax.shard_map(
        shards,
        mesh=mesh,
        in_specs=(
            P(("groups", "blk"), None),
            P(("groups", "blk"), None, "sector", None, None),
            P(("groups", "blk"), None, "sector"),
            P(("groups", "blk"), "sector", None, None),
            P(("groups", "blk")),
            P(("groups", "blk")),
        ),
        out_specs=(P(("groups", "blk", "sector"), None), P("groups")),
        check_vma=False,
    )
```
